32 devices in a mesh: groups: 2 (over y), patch: 8 (over z, x), heads: 2 (over core).
Axes of the slice: x: 2, y: 2, z: 4, core: 2. Of those that a mesh axis runs over, the one named last changes fastest.
Arguments:
- hidden_in: bfloat16 [512, 1280], P(('groups', 'patch'), 'heads'), parts along dimension 0, may hold values from -150 to 150
- gn_gain: float32 [1280], P('heads'), may hold values from 0.25 to 1.75
- gn_bias: float32 [1280], P('heads'), may hold values from -3 to 3
- w_in: bfloat16 [1280, 1280], P(None, 'heads'), may hold values from -0.15625 to 0.15625
- b_in: float32 [1280], P('heads'), may hold values from -3 to 3
- ln_gain: float32 [1280], replicated, may hold values from 0.25 to 1.75
- ln_bias: float32 [1280], replicated, may hold values from -3 to 3
- w_qkv: bfloat16 [3, 1280, 1280], P(None, None, 'heads'), may hold values from -0.15625 to 0.15625
- stale_kv: bfloat16 [2, 512, 1280], P(None, ('groups', 'patch'), 'heads'), parts along dimension 1, may hold values from -64 to 64
- w_out: bfloat16 [1280, 1280], P('heads'), may hold values from -0.15625 to 0.15625
- b_out: float32 [1280], P('heads'), may hold values from -3 to 3
Outputs:
- hidden_out: float32 [512, 1280], P(('groups', 'patch'), 'heads'), parts along dimension 0
The draws below stay inside these ranges and needn't reach their ends.
There are 2 independent parts, one for each index of `groups`. The reference program is written for one: setup_inputs(seed, part) draws one part's arguments, and reference() takes and returns one part's arrays. A program takes and returns all parts, laid end to end along the dimension named above; an argument that names none is the same for every part. Nothing has to cross between parts.
All inputs are finite; a program needn't handle non-finite values.
Results may differ from the reference program's by a relative error of at most 0.035.
Values may be sent and summed in bfloat16 or wider, within the bound.
A program may use at most 128 MiB of HBM per device.

```python
import math
import jax
import jax.numpy as jnp
from jax import lax

C = 1280
HEADS = 20
HD = 64
GROUPS = 32
ROW_TOK = 32
TOKENS = 256
N_PATCH = 8


def draw_hidden_in(key, part):
    k_noise = jax.random.fold_in(key, 0)
    k_token = jax.random.fold_in(key, 1)
    k_chan = jax.random.fold_in(key, 2)
    k_offset = jax.random.fold_in(key, 4)
    k_osign = jax.random.fold_in(key, 5)
    noise = jnp.clip(jax.random.normal(k_noise, (TOKENS, C), jnp.float32), -4.0, 4.0)
    tok_scale = jnp.exp(jax.random.uniform(k_token, (TOKENS, GROUPS), jnp.float32, 0.0, math.log(10.0))) / 3.0
    tok_scale = jnp.repeat(tok_scale, C // GROUPS, axis=1)
    row_trend = jnp.exp(math.log(3.0) * jnp.arange(TOKENS, dtype=jnp.float32) / (TOKENS - 1)) / math.sqrt(3.0)
    chan_scale = jnp.exp(jax.random.uniform(k_chan, (C,), jnp.float32, math.log(0.4), math.log(4.0)))
    values = noise * tok_scale * row_trend[:, None] * chan_scale[None, :]
    offset_size = jax.random.uniform(k_offset, (GROUPS,), jnp.float32, 2.0, 5.0)
    offset_sign = jnp.where(jax.random.bernoulli(k_osign, 0.5, (GROUPS,)), 1.0, -1.0)
    group_offset = jnp.repeat(offset_size * offset_sign, C // GROUPS)
    position = jnp.arange(TOKENS, dtype=jnp.float32) / (TOKENS - 1)
    ramp = 0.2 + 0.8 * position
    values = values + ramp[:, None] * group_offset[None, :]
    return values.astype(jnp.bfloat16)


def draw_stale_kv(key, part):
    k_noise, k_scale = jax.random.split(key, 2)
    noise = jnp.clip(jax.random.normal(k_noise, (2, TOKENS, HEADS * HD), jnp.float32), -4.0, 4.0)
    tok_scale = jnp.exp(jax.random.uniform(k_scale, (2, TOKENS, HEADS), jnp.float32, math.log(0.5), math.log(3.0)))
    values = noise * jnp.repeat(tok_scale, HD, axis=2)
    return values.astype(jnp.bfloat16)


def block_scale(key, dims, cuts, low, largest):
    factor_of = 1.0
    for dim, parts in cuts:
        steps = jax.random.uniform(jax.random.fold_in(jax.random.fold_in(key, 6), dim), (parts,), jnp.float32, low / len(cuts), largest / len(cuts))
        factor_of = factor_of * jnp.repeat(jnp.exp(steps), dims[dim] // parts).reshape((-1,) + (1,) * (len(dims) - 1 - dim))
    return factor_of


def gaussian(stream_key, shape, width, bound, pieces=(), kind=jnp.bfloat16):
    drawn = width * jax.random.normal(stream_key, shape, jnp.float32)
    if pieces:
        drawn = drawn * block_scale(stream_key, shape, pieces, -0.22, 0.18)
    return jnp.clip(drawn, -bound, bound).astype(kind)


def setup_inputs(seed: int = 0, part: int = 0) -> dict:
    arg_keys = jax.random.split(jax.random.key(seed), 12)
    own_keys = jax.random.split(jax.random.fold_in(arg_keys[11], part), 12)
    return {
        "hidden_in": draw_hidden_in(jax.random.fold_in(jax.random.fold_in(arg_keys[11], part), 71), part),
        "gn_gain": jnp.clip(1.0 + 0.15 * jax.random.normal(arg_keys[1], (C,), jnp.float32), 0.25, 1.75),
        "gn_bias": gaussian(arg_keys[2], (C,), 0.5, 3.0, ((0, 2),), jnp.float32),
        "w_in": gaussian(arg_keys[3], (C, C), C ** -0.5, 0.15625, ((1, 2),)),
        "b_in": gaussian(arg_keys[4], (C,), 0.5, 3.0, ((0, 2),), jnp.float32),
        "ln_gain": jnp.clip(1.0 + 0.15 * jax.random.normal(arg_keys[5], (C,), jnp.float32), 0.25, 1.75),
        "ln_bias": gaussian(arg_keys[6], (C,), 0.5, 3.0, (), jnp.float32),
        "w_qkv": gaussian(arg_keys[7], (3, C, HEADS * HD), C ** -0.5, 0.15625, ((2, 2),)),
        "stale_kv": draw_stale_kv(jax.random.fold_in(jax.random.fold_in(arg_keys[11], part), 71), part),
        "w_out": gaussian(arg_keys[9], (HEADS * HD, C), (HEADS * HD) ** -0.5, 0.15625, ((0, 2),)),
        "b_out": gaussian(arg_keys[10], (C,), 0.5, 3.0, ((0, 2),), jnp.float32),
    }


def to_float(array):
    return lax.optimization_barrier(array).astype(jnp.float32)

def reference(hidden_in, gn_gain, gn_bias, w_in, b_in, ln_gain, ln_bias, w_qkv, stale_kv, w_out, b_out):
    group_size = C // GROUPS
    values = hidden_in.astype(jnp.float32).reshape(TOKENS, GROUPS, group_size)
    grp_mean = lax.optimization_barrier(jnp.mean(values, axis=(0, 2)))
    centered = values - grp_mean[None, :, None]
    grp_var = lax.optimization_barrier(jnp.mean(centered * centered, axis=(0, 2)))
    normed = (centered * lax.rsqrt(grp_var + 1e-06)[None, :, None]).reshape(TOKENS, C) * gn_gain + gn_bias
    normed = normed.astype(jnp.bfloat16)
    stream = (jnp.dot(normed, w_in, preferred_element_type=jnp.float32) + b_in).astype(jnp.bfloat16)
    stream_float = stream.astype(jnp.float32)
    tok_mean = lax.optimization_barrier(jnp.mean(stream_float, axis=1, keepdims=True))
    tok_centered = stream_float - tok_mean
    tok_var = lax.optimization_barrier(jnp.mean(tok_centered * tok_centered, axis=1, keepdims=True))
    layer_normed = (tok_centered * lax.rsqrt(tok_var + 1e-05) * ln_gain + ln_bias).astype(jnp.bfloat16)
    projections = jnp.einsum('tc,icd->itd', to_float(layer_normed), w_qkv.astype(jnp.float32)).astype(jnp.bfloat16)
    projections = to_float(projections)
    all_query = projections[0].reshape(N_PATCH, ROW_TOK, HEADS, HD)
    all_key = projections[1].reshape(N_PATCH, ROW_TOK, HEADS, HD)
    all_val = projections[2].reshape(N_PATCH, ROW_TOK, HEADS, HD)
    stale_keys = stale_kv[0].astype(jnp.float32).reshape(TOKENS, HEADS, HD)
    stale_vals = stale_kv[1].astype(jnp.float32).reshape(TOKENS, HEADS, HD)

    def attend_strip(strip_args):
        strip_idx, strip_query, strip_key, strip_val = strip_args
        first_row = (strip_idx * ROW_TOK).astype(jnp.int32)
        zero_idx = jnp.zeros((), jnp.int32)
        key_rows = lax.dynamic_update_slice(stale_keys, strip_key, (first_row, zero_idx, zero_idx))
        val_rows = lax.dynamic_update_slice(stale_vals, strip_val, (first_row, zero_idx, zero_idx))
        scores = jnp.einsum('whd,thd->wht', strip_query, key_rows) * HD ** (-0.5)
        row_max = lax.optimization_barrier(jnp.max(scores, axis=-1, keepdims=True))
        weights = jnp.exp(scores - row_max)
        weight_sum = lax.optimization_barrier(jnp.sum(weights, axis=-1))
        out_sum = jnp.einsum('wht,thd->whd', to_float(weights.astype(jnp.bfloat16)), val_rows)
        return (out_sum / weight_sum[..., None]).astype(jnp.bfloat16)
    attended = lax.map(attend_strip, (jnp.arange(N_PATCH, dtype=jnp.int32), all_query, all_key, all_val))
    attended = attended.reshape(TOKENS, HEADS * HD)
    head_terms = jnp.dot(attended, w_out, preferred_element_type=jnp.float32) + b_out
    return stream_float + head_terms
```

```python
import functools
import jax
import jax.numpy as jnp
from jax import lax
from jax.experimental import pallas as pl
from jax.experimental.pallas import tpu as pltpu
from jax.sharding import PartitionSpec as P

HD = 64
GROUPS = 32
LANES = 128
MESH = pl.DeviceIdType.MESH
F32 = jnp.float32
BF16 = jnp.bfloat16


def each(first, last, action):
    if last - first <= 16:
        for index in range(first, last):
            action(index)
    else:

        def step(index, carry):
            action(index)
            return carry

        lax.fori_loop(first, last, step, 0)


def dot(a, b):
    return jnp.dot(a, b, preferred_element_type=F32)


def exact_dot(a, b):
    return jnp.dot(a, b, preferred_element_type=F32, precision=lax.Precision.HIGHEST)


def kernel(
    n,
    hidden_hbm, gain_hbm, bias_hbm, w_in_hbm, b_in_hbm, ln_gain_hbm, ln_bias_hbm,
    w_qkv_hbm, stale_hbm, w_out_hbm, b_out_hbm,
    out_ref,
    hidden, gain, bias, affine, w_in, b_in, ln_gain, ln_bias, w_qkv, w_out, b_out,
    stats_src, stats, kv, stream, terms,
    local_sem, stats_send, stats_recv, kv_send, kv_recv, pair_send, pair_recv,
):
    p = lax.axis_index("patch")
    h = lax.axis_index("heads")
    rows, half = hidden.shape[1:]
    width = 2 * half
    group_size = width // GROUPS
    cells = float(rows * n * group_size)

    def row(ref):
        return ref[...].reshape(1, -1)

    def halves(ref):
        whole = row(ref)
        low, high = whole[:, :half], whole[:, half:]
        return jnp.where(h == 0, low, high), jnp.where(h == 0, high, low)

    locals_ = []

    def fetch(src, dst):
        copy = pltpu.make_async_copy(src, dst, local_sem.at[len(locals_)])
        copy.start()
        locals_.append(copy)
        return copy

    get_hidden = fetch(hidden_hbm, hidden.at[0])

    barrier = pltpu.get_barrier_semaphore()

    def peer(d, k):
        return {"patch": lax.rem(p + d, n), "heads": h if k == 0 else 1 - h}

    def greet(k):
        def action(d):
            pl.semaphore_signal(barrier, inc=1, device_id=peer(d, k), device_id_type=MESH)

        return action

    each(1, n, greet(0))
    each(0, n, greet(1))

    get_gain = fetch(gain_hbm, gain)
    get_bias = fetch(bias_hbm, bias)
    get_b_in = fetch(b_in_hbm, b_in)
    get_w_in = fetch(w_in_hbm, w_in)
    get_ln_gain = fetch(ln_gain_hbm, ln_gain)
    get_ln_bias = fetch(ln_bias_hbm, ln_bias)
    get_qkv = [fetch(w_qkv_hbm.at[i], w_qkv.at[i]) for i in range(3)]
    get_w_out = [
        fetch(
            w_out_hbm.at[:, pl.ds(pl.multiple_of((h if k == 0 else 1 - h) * half, LANES), half)],
            w_out.at[k],
        )
        for k in (1, 0)
    ]
    get_b_out = fetch(b_out_hbm, b_out)

    chan = lax.broadcasted_iota(jnp.int32, (half, LANES), 0)
    edge = lax.broadcasted_iota(jnp.int32, (half, LANES), 1) * group_size
    to_group = ((chan >= edge) & (chan < edge + group_size)).astype(F32)
    chan = lax.broadcasted_iota(jnp.int32, (LANES, half), 1)
    edge = lax.broadcasted_iota(jnp.int32, (LANES, half), 0) * group_size
    from_group = ((chan >= edge) & (chan < edge + group_size)).astype(F32)

    get_hidden.wait()
    own = hidden[0].astype(F32)
    sums = jnp.concatenate(
        [
            jnp.sum(own, axis=0, keepdims=True),
            jnp.sum(own * own, axis=0, keepdims=True),
            jnp.zeros((6, half), F32),
        ],
        axis=0,
    )
    own_stats = exact_dot(sums, to_group)
    stats_src[...] = own_stats
    stats[0, 0] = own_stats
    get_gain.wait()
    get_bias.wait()
    affine[0, 0:1] = row(gain)
    affine[0, 1:2] = row(bias)

    pl.semaphore_wait(barrier, 2 * n - 1)

    def send_stats(k):
        def action(d):
            pltpu.make_async_remote_copy(
                src_ref=stats_src, dst_ref=stats.at[k, d],
                send_sem=stats_send.at[k], recv_sem=stats_recv.at[k],
                device_id=peer(d, k), device_id_type=MESH,
            ).start()

        return action

    each(1, n, send_stats(0))
    each(0, n, send_stats(1))

    def to_partner(index, src, dst):
        copy = pltpu.make_async_remote_copy(
            src_ref=src, dst_ref=dst,
            send_sem=pair_send.at[index], recv_sem=pair_recv.at[index],
            device_id=peer(0, 1), device_id_type=MESH,
        )
        copy.start()
        return copy

    swap_hidden = to_partner(0, hidden_hbm, hidden.at[1])
    swap_affine = to_partner(1, affine.at[0], affine.at[1])

    def send_kv(d):
        pltpu.make_async_remote_copy(
            src_ref=stale_hbm, dst_ref=kv.at[:, d],
            send_sem=kv_send, recv_sem=kv_recv,
            device_id=peer(d, 0), device_id_type=MESH,
        ).start()

    each(1, n, send_kv)

    def all_of(ref, send_sem, recv_sem):
        return pltpu.make_async_remote_copy(
            src_ref=ref, dst_ref=ref, send_sem=send_sem, recv_sem=recv_sem,
            device_id=peer(0, 1), device_id_type=MESH,
        )

    all_stats = [
        all_of(stats.at[0, pl.ds(1, n - 1)], stats_send.at[0], stats_recv.at[0]),
        all_of(stats.at[1], stats_send.at[1], stats_recv.at[1]),
    ]
    all_kv = all_of(kv.at[:, pl.ds(1, n - 1)], kv_send, kv_recv)

    swap_hidden.wait_recv()
    swap_affine.wait_recv()
    get_b_in.wait()
    get_w_in.wait()
    all_stats[0].wait_recv()
    all_stats[1].wait_recv()

    per_group = []
    for k in range(2):
        total = jnp.sum(stats[k], axis=0) / cells
        mean = total[0:1]
        per_group += [mean, lax.rsqrt(total[1:2] - mean * mean + 1e-06)]
    per_group.append(jnp.zeros((4, LANES), F32))
    per_chan = exact_dot(jnp.concatenate(per_group, axis=0), from_group)

    projected = row(b_in)
    for k in range(2):
        values = hidden[k].astype(F32)
        mean, scale = per_chan[2 * k : 2 * k + 1], per_chan[2 * k + 1 : 2 * k + 2]
        normed = ((values - mean) * scale * affine[k, 0:1] + affine[k, 1:2]).astype(BF16)
        projected = projected + dot(normed, w_in[h if k == 0 else 1 - h])
    stream[0] = projected.astype(BF16)
    swap_stream = to_partner(2, stream.at[0], stream.at[1])

    get_ln_gain.wait()
    get_ln_bias.wait()
    gains, biases = halves(ln_gain), halves(ln_bias)
    for copy in get_qkv:
        copy.wait()
    own = stream[0].astype(F32)
    own_total = jnp.sum(own, axis=1, keepdims=True)
    swap_stream.wait_recv()
    other = stream[1].astype(F32)
    tok_mean = (own_total + jnp.sum(other, axis=1, keepdims=True)) / width
    own = own - tok_mean
    other = other - tok_mean
    squares = jnp.sum(own * own, axis=1, keepdims=True) + jnp.sum(
        other * other, axis=1, keepdims=True
    )
    tok_scale = lax.rsqrt(squares / width + 1e-05)
    own = (own * tok_scale * gains[0] + biases[0]).astype(BF16)
    other = (other * tok_scale * gains[1] + biases[1]).astype(BF16)

    def project(i):
        return dot(own, w_qkv[i, h]) + dot(other, w_qkv[i, 1 - h])

    queries = project(0)
    kv[0, 0] = project(1).astype(BF16)
    kv[1, 0] = project(2).astype(BF16)
    all_kv.wait_recv()

    first_head = lax.broadcasted_iota(jnp.int32, (rows, LANES), 1) < HD
    attended = []
    for first in range(0, half, LANES):
        lanes = slice(first, first + LANES)
        query = queries[:, lanes]
        both = jnp.concatenate(
            [jnp.where(first_head, query, 0.0), jnp.where(first_head, 0.0, query)], axis=0
        ).astype(BF16)
        keys = kv[0, :, :, lanes].reshape(n * rows, LANES)
        vals = kv[1, :, :, lanes].reshape(n * rows, LANES)
        scores = lax.dot_general(
            both, keys, (((1,), (1,)), ((), ())), preferred_element_type=F32
        ) * HD ** (-0.5)
        weights = jnp.exp(scores - jnp.max(scores, axis=1, keepdims=True))
        weight_sum = jnp.sum(weights, axis=1, keepdims=True)
        mixed = dot(weights.astype(BF16), vals) / weight_sum
        attended.append(jnp.where(first_head, mixed[:rows], mixed[rows:]).astype(BF16))
    attended = jnp.concatenate(attended, axis=1)

    for copy in get_w_out:
        copy.wait()
    terms[0] = dot(attended, w_out[1])
    swap_terms = to_partner(3, terms.at[0], terms.at[1])
    get_b_out.wait()
    result = stream[0].astype(F32) + row(b_out) + dot(attended, w_out[0])
    swap_terms.wait_recv()
    out_ref[...] = result + terms[1]

    for copy in (swap_hidden, swap_affine, swap_stream, swap_terms):
        copy.wait_send()
    all_stats[0].wait_send()
    all_stats[1].wait_send()
    all_kv.wait_send()


def body(n, hidden_in, gn_gain, gn_bias, w_in, b_in, ln_gain, ln_bias, w_qkv, stale_kv, w_out, b_out):
    rows, half = hidden_in.shape
    width = ln_gain.shape[0]
    return pl.pallas_call(
        functools.partial(kernel, n),
        out_shape=jax.ShapeDtypeStruct((rows, half), F32),
        in_specs=[pl.BlockSpec(memory_space=pl.ANY)] * 11,
        out_specs=pl.BlockSpec(memory_space=pltpu.VMEM),
        scratch_shapes=[
            pltpu.VMEM((2, rows, half), BF16),
            pltpu.VMEM((half,), F32),
            pltpu.VMEM((half,), F32),
            pltpu.VMEM((2, 2, half), F32),
            pltpu.VMEM((2, half, half), BF16),
            pltpu.VMEM((half,), F32),
            pltpu.VMEM((width,), F32),
            pltpu.VMEM((width,), F32),
            pltpu.VMEM((3, 2, half, half), BF16),
            pltpu.VMEM((2, half, half), BF16),
            pltpu.VMEM((half,), F32),
            pltpu.VMEM((8, LANES), F32),
            pltpu.VMEM((2, n, 8, LANES), F32),
            pltpu.VMEM((2, n, rows, half), BF16),
            pltpu.VMEM((2, rows, half), BF16),
            pltpu.VMEM((2, rows, half), F32),
            pltpu.SemaphoreType.DMA((13,)),
            pltpu.SemaphoreType.DMA((2,)),
            pltpu.SemaphoreType.DMA((2,)),
            pltpu.SemaphoreType.DMA,
            pltpu.SemaphoreType.DMA,
            pltpu.SemaphoreType.DMA((4,)),
            pltpu.SemaphoreType.DMA((4,)),
        ],
        compiler_params=pltpu.CompilerParams(
            collective_id=0, has_side_effects=True, vmem_limit_bytes=56 * 2**20
        ),
    )(
        hidden_in,
        gn_gain,
        gn_bias,
        w_in.reshape(2, half, half),
        b_in,
        ln_gain,
        ln_bias,
        w_qkv.reshape(3, 2, half, half),
        stale_kv,
        w_out,
        b_out,
    )


def solution(mesh):
    placed = (
        P(("groups", "patch"), "heads"),
        P("heads"),
        P("heads"),
        P(None, "heads"),
        P("heads"),
        P(),
        P(),
        P(None, None, "heads"),
        P(None, ("groups", "patch"), "heads"),
        P("heads", None),
        P("heads"),
    )
    return jax.shard_map(
        functools.partial(body, mesh.shape["patch"]),
        mesh=mesh,
        in_specs=placed,
        out_specs=P(("groups", "patch"), "heads"),
        check_vma=False,
    )
```

```python
import functools
import jax
import jax.numpy as jnp
from jax import lax
from jax.experimental import pallas as pl
from jax.experimental.pallas import tpu as pltpu
from jax.sharding import PartitionSpec as P

HD = 64
GROUPS = 32
LANES = 128
MESH = pl.DeviceIdType.MESH
F32 = jnp.float32
BF16 = jnp.bfloat16


def each(first, last, action):
    if last - first <= 16:
        for index in range(first, last):
            action(index)
    else:

        def step(index, carry):
            action(index)
            return carry

        lax.fori_loop(first, last, step, 0)


def dot(a, b):
    return jnp.dot(a, b, preferred_element_type=F32)


def exact_dot(a, ones):
    high = a.astype(BF16).astype(F32)
    rest = a - high
    middle = rest.astype(BF16).astype(F32)
    terms = jnp.concatenate([high, middle, rest - middle], axis=0).astype(BF16)
    sums = dot(terms, ones)
    count = a.shape[0]
    return sums[:count] + sums[count : 2 * count] + sums[2 * count :]


def kernel(
    n,
    hidden_hbm, gain_hbm, bias_hbm, w_in_hbm, b_in_hbm, ln_gain_hbm, ln_bias_hbm,
    w_qkv_hbm, stale_hbm, w_out_hbm, b_out_hbm,
    out_ref,
    hidden, gain, bias, affine, w_in, b_in, ln_gain, ln_bias, w_qkv, w_out, b_out,
    stats_src, stats, kv, stream, terms,
    local_sem, stats_send, stats_recv, kv_send, kv_recv, pair_send, pair_recv,
):
    p = lax.axis_index("patch")
    h = lax.axis_index("heads")
    rows, half = hidden.shape[1:]
    width = 2 * half
    group_size = width // GROUPS
    cells = float(rows * n * group_size)

    def row(ref):
        return ref[...].reshape(1, -1)

    def halves(ref):
        whole = row(ref)
        low, high = whole[:, :half], whole[:, half:]
        return jnp.where(h == 0, low, high), jnp.where(h == 0, high, low)

    locals_ = []

    def fetch(src, dst):
        copy = pltpu.make_async_copy(src, dst, local_sem.at[len(locals_)])
        copy.start()
        locals_.append(copy)
        return copy

    get_hidden = fetch(hidden_hbm, hidden.at[0])

    barrier = pltpu.get_barrier_semaphore()

    def peer(d, k):
        return {"patch": lax.rem(p + d, n), "heads": h if k == 0 else 1 - h}

    def greet(k):
        def action(d):
            pl.semaphore_signal(barrier, inc=1, device_id=peer(d, k), device_id_type=MESH)

        return action

    each(1, n, greet(0))
    each(0, n, greet(1))

    get_gain = fetch(gain_hbm, gain)
    get_bias = fetch(bias_hbm, bias)
    get_b_in = fetch(b_in_hbm, b_in)
    get_w_in = fetch(w_in_hbm, w_in)
    get_ln_gain = fetch(ln_gain_hbm, ln_gain)
    get_ln_bias = fetch(ln_bias_hbm, ln_bias)
    get_qkv = [fetch(w_qkv_hbm.at[i], w_qkv.at[i]) for i in range(3)]
    get_w_out = [
        fetch(
            w_out_hbm.at[:, pl.ds(pl.multiple_of((h if k == 0 else 1 - h) * half, LANES), half)],
            w_out.at[k],
        )
        for k in (1, 0)
    ]
    get_b_out = fetch(b_out_hbm, b_out)

    chan = lax.broadcasted_iota(jnp.int32, (half, LANES), 0)
    edge = lax.broadcasted_iota(jnp.int32, (half, LANES), 1) * group_size
    to_group = ((chan >= edge) & (chan < edge + group_size)).astype(F32).astype(BF16)
    chan = lax.broadcasted_iota(jnp.int32, (LANES, half), 1)
    edge = lax.broadcasted_iota(jnp.int32, (LANES, half), 0) * group_size
    from_group = ((chan >= edge) & (chan < edge + group_size)).astype(F32).astype(BF16)

    get_hidden.wait()
    own = hidden[0].astype(F32)
    sums = jnp.concatenate(
        [
            jnp.sum(own, axis=0, keepdims=True),
            jnp.sum(own * own, axis=0, keepdims=True),
            jnp.zeros((6, half), F32),
        ],
        axis=0,
    )
    own_stats = exact_dot(sums, to_group)
    stats_src[...] = own_stats
    stats[0, 0] = own_stats
    get_gain.wait()
    get_bias.wait()
    affine[0, 0:1] = row(gain)
    affine[0, 1:2] = row(bias)

    pl.semaphore_wait(barrier, 2 * n - 1)

    def send_stats(k):
        def action(d):
            pltpu.make_async_remote_copy(
                src_ref=stats_src, dst_ref=stats.at[k, d],
                send_sem=stats_send.at[k], recv_sem=stats_recv.at[k],
                device_id=peer(d, k), device_id_type=MESH,
            ).start()

        return action

    each(1, n, send_stats(0))
    each(0, n, send_stats(1))

    def to_partner(index, src, dst):
        copy = pltpu.make_async_remote_copy(
            src_ref=src, dst_ref=dst,
            send_sem=pair_send.at[index], recv_sem=pair_recv.at[index],
            device_id=peer(0, 1), device_id_type=MESH,
        )
        copy.start()
        return copy

    swap_hidden = to_partner(0, hidden_hbm, hidden.at[1])
    swap_affine = to_partner(1, affine.at[0], affine.at[1])

    def all_of(ref, send_sem, recv_sem):
        return pltpu.make_async_remote_copy(
            src_ref=ref, dst_ref=ref, send_sem=send_sem, recv_sem=recv_sem,
            device_id=peer(0, 1), device_id_type=MESH,
        )

    two_level = n % 4 == 0 and n <= 16
    quad, place = p // 4, lax.rem(p, 4)

    def send_kv(source, target, ref):
        pltpu.make_async_remote_copy(
            src_ref=ref, dst_ref=kv.at[:, source],
            send_sem=kv_send, recv_sem=kv_recv.at[source],
            device_id={"patch": target, "heads": h}, device_id_type=MESH,
        ).start()

    def kv_arrived(source):
        all_of(kv.at[:, source], kv_send, kv_recv.at[source]).wait_recv()

    def place_in(other, step):
        return other * 4 + lax.rem(place + step, 4)

    def hand_on(source):
        kv_arrived(source)
        for step in (2, 1, 3):
            send_kv(source, place_in(quad, step), kv.at[:, source])

    others = [lax.rem(quad + step, n // 4) for step in range(1, n // 4)] if two_level else []
    if two_level:
        for other in others:
            send_kv(p, place_in(other, 0), stale_hbm)
        for step in (2, 1, 3):
            send_kv(p, place_in(quad, step), stale_hbm)
    else:
        each(1, n, lambda d: send_kv(p, lax.rem(p + d, n), stale_hbm))

    all_stats = [
        all_of(stats.at[0, pl.ds(1, n - 1)], stats_send.at[0], stats_recv.at[0]),
        all_of(stats.at[1], stats_send.at[1], stats_recv.at[1]),
    ]
    all_kv_sent = all_of(kv.at[:, pl.ds(1, n - 1)], kv_send, kv_recv.at[0])

    swap_hidden.wait_recv()
    swap_affine.wait_recv()
    get_b_in.wait()
    get_w_in.wait()
    all_stats[0].wait_recv()
    all_stats[1].wait_recv()

    per_group = []
    for k in range(2):
        total = jnp.sum(stats[k], axis=0) / cells
        mean = total[0:1]
        per_group += [mean, lax.rsqrt(total[1:2] - mean * mean + 1e-06)]
    per_group.append(jnp.zeros((4, LANES), F32))
    per_chan = exact_dot(jnp.concatenate(per_group, axis=0), from_group)

    projected = row(b_in)
    for k in range(2):
        values = hidden[k].astype(F32)
        mean, scale = per_chan[2 * k : 2 * k + 1], per_chan[2 * k + 1 : 2 * k + 2]
        normed = ((values - mean) * scale * affine[k, 0:1] + affine[k, 1:2]).astype(BF16)
        projected = projected + dot(normed, w_in[h if k == 0 else 1 - h])
    stream[0] = projected.astype(BF16)
    swap_stream = to_partner(2, stream.at[0], stream.at[1])

    get_ln_gain.wait()
    get_ln_bias.wait()
    gains, biases = halves(ln_gain), halves(ln_bias)
    for copy in get_qkv:
        copy.wait()
    own = stream[0].astype(F32)
    own_total = jnp.sum(own, axis=1, keepdims=True)
    for other in others:
        hand_on(place_in(other, 0))
    swap_stream.wait_recv()
    other = stream[1].astype(F32)
    tok_mean = (own_total + jnp.sum(other, axis=1, keepdims=True)) / width
    own = own - tok_mean
    other = other - tok_mean
    squares = jnp.sum(own * own, axis=1, keepdims=True) + jnp.sum(
        other * other, axis=1, keepdims=True
    )
    tok_scale = lax.rsqrt(squares / width + 1e-05)
    own = (own * tok_scale * gains[0] + biases[0]).astype(BF16)
    other = (other * tok_scale * gains[1] + biases[1]).astype(BF16)

    def project(i):
        return dot(own, w_qkv[i, h]) + dot(other, w_qkv[i, 1 - h])

    queries = project(0)
    kv[0, p] = project(1).astype(BF16)
    kv[1, p] = project(2).astype(BF16)
    if two_level:
        for other in [quad] + others:
            for step in (2, 1, 3):
                kv_arrived(place_in(other, step))
    else:
        each(1, n, lambda d: kv_arrived(lax.rem(p + d, n)))

    first_head = lax.broadcasted_iota(jnp.int32, (rows, LANES), 1) < HD
    attended = []
    for first in range(0, half, LANES):
        lanes = slice(first, first + LANES)
        query = queries[:, lanes]
        both = jnp.concatenate(
            [jnp.where(first_head, query, 0.0), jnp.where(first_head, 0.0, query)], axis=0
        ).astype(BF16)
        keys = kv[0, :, :, lanes].reshape(n * rows, LANES)
        vals = kv[1, :, :, lanes].reshape(n * rows, LANES)
        scores = lax.dot_general(
            both, keys, (((1,), (1,)), ((), ())), preferred_element_type=F32
        ) * HD ** (-0.5)
        weights = jnp.exp(scores - jnp.max(scores, axis=1, keepdims=True))
        weight_sum = jnp.sum(weights, axis=1, keepdims=True)
        mixed = dot(weights.astype(BF16), vals) / weight_sum
        attended.append(jnp.where(first_head, mixed[:rows], mixed[rows:]).astype(BF16))
    attended = jnp.concatenate(attended, axis=1)

    for copy in get_w_out:
        copy.wait()
    terms[0] = dot(attended, w_out[1])
    swap_terms = to_partner(3, terms.at[0], terms.at[1])
    get_b_out.wait()
    result = stream[0].astype(F32) + row(b_out) + dot(attended, w_out[0])
    swap_terms.wait_recv()
    out_ref[...] = result + terms[1]

    for copy in (swap_hidden, swap_affine, swap_stream, swap_terms):
        copy.wait_send()
    all_stats[0].wait_send()
    all_stats[1].wait_send()
    all_kv_sent.wait_send()


def body(n, hidden_in, gn_gain, gn_bias, w_in, b_in, ln_gain, ln_bias, w_qkv, stale_kv, w_out, b_out):
    rows, half = hidden_in.shape
    width = ln_gain.shape[0]
    return pl.pallas_call(
        functools.partial(kernel, n),
        out_shape=jax.ShapeDtypeStruct((rows, half), F32),
        in_specs=[pl.BlockSpec(memory_space=pl.ANY)] * 11,
        out_specs=pl.BlockSpec(memory_space=pltpu.VMEM),
        scratch_shapes=[
            pltpu.VMEM((2, rows, half), BF16),
            pltpu.VMEM((half,), F32),
            pltpu.VMEM((half,), F32),
            pltpu.VMEM((2, 2, half), F32),
            pltpu.VMEM((2, half, half), BF16),
            pltpu.VMEM((half,), F32),
            pltpu.VMEM((width,), F32),
            pltpu.VMEM((width,), F32),
            pltpu.VMEM((3, 2, half, half), BF16),
            pltpu.VMEM((2, half, half), BF16),
            pltpu.VMEM((half,), F32),
            pltpu.VMEM((8, LANES), F32),
            pltpu.VMEM((2, n, 8, LANES), F32),
            pltpu.VMEM((2, n, rows, half), BF16),
            pltpu.VMEM((2, rows, half), BF16),
            pltpu.VMEM((2, rows, half), F32),
            pltpu.SemaphoreType.DMA((13,)),
            pltpu.SemaphoreType.DMA((2,)),
            pltpu.SemaphoreType.DMA((2,)),
            pltpu.SemaphoreType.DMA,
            pltpu.SemaphoreType.DMA((n,)),
            pltpu.SemaphoreType.DMA((4,)),
            pltpu.SemaphoreType.DMA((4,)),
        ],
        compiler_params=pltpu.CompilerParams(
            collective_id=0, has_side_effects=True, vmem_limit_bytes=56 * 2**20
        ),
    )(
        hidden_in,
        gn_gain,
        gn_bias,
        w_in.reshape(2, half, half),
        b_in,
        ln_gain,
        ln_bias,
        w_qkv.reshape(3, 2, half, half),
        stale_kv,
        w_out,
        b_out,
    )


def solution(mesh):
    placed = (
        P(("groups", "patch"), "heads"),
        P("heads"),
        P("heads"),
        P(None, "heads"),
        P("heads"),
        P(),
        P(),
        P(None, None, "heads"),
        P(None, ("groups", "patch"), "heads"),
        P("heads", None),
        P("heads"),
    )
    return jax.shard_map(
        functools.partial(body, mesh.shape["patch"]),
        mesh=mesh,
        in_specs=placed,
        out_specs=P(("groups", "patch"), "heads"),
        check_vma=False,
    )
```
